512 devices in a mesh: node: 16 (over x, z_hi), local: 32 (over z_lo, y, core).
Axes of the slice: x: 4, y: 4, z: 16 (z_hi: 4, z_lo: 4; z = z_hi * 4 + z_lo), core: 2. Of those that a mesh axis runs over, the one named last changes fastest.
Arguments:
- activations: bfloat16 [98304, 2560], P(('node', 'local')), may hold values from -0.078125 to 0.078125
- out_grad: bfloat16 [98304, 512], P(('node', 'local')), may hold values from -6 to 6
- key_weight: bfloat16 [2560, 512], P('local'), may hold values from -0.125 to 0.125
Outputs:
- input_grad: bfloat16 [98304, 2560], P(('node', 'local'))
- weight_grad: float32 [2560, 512], P(('node', 'local'))
The draws below stay inside these ranges and needn't reach their ends.
All inputs are finite; a program needn't handle non-finite values.
Results may differ from the reference program's by a relative error of at most 0.0049.
Values may be sent and summed in bfloat16 or wider, within the bound.
No kernel may reach another device: no remote copies, remote signals or barrier semaphores. Data moves between devices by JAX's collectives and lax.ppermute only.
A program may use at most 128 MiB of HBM per device.

```python
import jax
import jax.numpy as jnp
from jax import lax

D = 2560
KV = 512
BLOCK = 256
TOK_DEV = 192
TOKENS = 98304
N_NODE = 16
N_LOCAL = 32


def strengthened(values, own_key, source, target, blocks, factor):
    def block_of(dim):
        return (jnp.arange(values.shape[dim]) // (values.shape[dim] // blocks)).reshape((-1,) + (1,) * (values.ndim - 1 - dim))

    first = jax.random.permutation(own_key, blocks)[block_of(target)]
    second = (block_of(target) + blocks // 2) % blocks
    return jnp.where((block_of(source) == first) | (block_of(source) == second), factor * values, values)


def level_of(key, shape, pieces, low, top_value):
    def one(axis_at, shards_of):
        heights = jax.random.uniform(jax.random.fold_in(jax.random.fold_in(key, 6), axis_at), (shards_of,), jnp.float32, low / len(pieces), top_value / len(pieces))
        return jnp.repeat(jnp.exp(heights), shape[axis_at] // shards_of).reshape((-1,) + (1,) * (len(shape) - axis_at - 1))

    gain = one(*pieces[0])
    for cut in pieces[1:]:
        gain = gain * one(*cut)
    return gain


def scatter_about(rng, shape, width, bound, pieces=(), held_as=jnp.bfloat16):
    array = width * jax.random.normal(rng, shape, jnp.float32)
    if pieces:
        array = array * level_of(rng, shape, pieces, -0.22, 0.18)
    return jnp.clip(array, -bound, bound).astype(held_as)


def gaussian_with(rng, extent, scale, limit, shards, heavy, kind=jnp.bfloat16):
    result = scale * jax.random.normal(rng, extent, jnp.float32)
    if shards:
        result = result * level_of(rng, extent, shards, -0.22, 0.18)
    return jnp.clip(strengthened(result, jax.random.fold_in(rng, 3), *heavy), -limit, limit).astype(kind)


def setup_inputs(seed: int = 0) -> dict:
    splits = jax.random.split(jax.random.key(seed), 4)
    activations = gaussian_with(splits[0], (TOKENS, D), ((TOKENS) ** -0.5), 0.078125, ((0, 512),), (0, 1, 512, 6.0))
    out_grad = scatter_about(splits[1], (TOKENS, KV), 1.0, 6.0, ((0, 512),))
    key_weight = scatter_about(splits[2], (D, KV), D ** -0.5, 0.125, ((0, 32),))
    return {"activations": activations, "out_grad": out_grad, "key_weight": key_weight}


def encode_blocks(grad):
    blocks = grad.reshape(grad.shape[:-1] + (grad.shape[-1] // BLOCK, BLOCK))
    scales = (jnp.max(jnp.abs(blocks), axis=-1) / 7.0 + 1e-6).astype(jnp.bfloat16)
    coded = (blocks / scales.astype(jnp.float32)[..., None]).astype(jnp.bfloat16)
    return coded.reshape(grad.shape), scales


def decode_blocks(coded, scales):
    blocks = coded.astype(jnp.float32).reshape(coded.shape[:-1] + (coded.shape[-1] // BLOCK, BLOCK))
    return (blocks * scales.astype(jnp.float32)[..., None]).reshape(coded.shape)


def reference(activations, out_grad, key_weight):
    grad_blocks = out_grad.reshape(N_NODE * N_LOCAL, TOK_DEV, KV)

    def input_block(block):
        return jnp.dot(block, key_weight.T, preferred_element_type=jnp.float32).astype(jnp.bfloat16)

    input_grad = lax.map(input_block, grad_blocks).reshape(TOKENS, D)
    act_groups = activations.reshape(N_NODE, N_LOCAL, TOK_DEV, D)
    grad_groups = out_grad.reshape(N_NODE, N_LOCAL, TOK_DEV, KV)

    def member_step(total, pair):
        partial_value = jnp.dot(pair[0].T, pair[1], preferred_element_type=jnp.float32)
        coded, scales = encode_blocks(partial_value)
        coded, scales = lax.optimization_barrier((coded, scales))
        return total + decode_blocks(coded, scales), None

    def group_step(total, pair):
        group_sum, unused = lax.scan(member_step, jnp.zeros((D, KV), jnp.float32), pair)
        coded, scales = encode_blocks(group_sum)
        coded, scales = lax.optimization_barrier((coded, scales))
        return total + decode_blocks(coded, scales), None

    weight_grad, unused = lax.scan(group_step, jnp.zeros((D, KV), jnp.float32), (act_groups, grad_groups))
    return input_grad, weight_grad
```

```python
import jax
import jax.numpy as jnp
from jax import lax
from jax.experimental import pallas as pl
from jax.experimental.pallas import tpu as pltpu
from jax.sharding import Mesh, PartitionSpec as P

X, ZH, ZL, Y, C = 4, 4, 4, 4, 2
Z = ZH * ZL
VMEM_LIMIT = 48 * 1024 * 1024

NT = (((1,), (1,)), ((), ()))
TN = (((0,), (0,)), ((), ()))


def dot(a, b, dims):
    return lax.dot_general(a, b, dims, preferred_element_type=jnp.float32)


def all_to_all(a, axes):
    return lax.all_to_all(a, axes, split_axis=0, concat_axis=0, tiled=True)


def shift(a, axes, step, size):
    return lax.ppermute(a, axes, [(i, (i + step) % size) for i in range(size)])


def pair_product(act, act_other, grad, grad_other, out):
    half = pl.ds(pl.multiple_of(lax.axis_index("c") * 256, 256), 256)
    total = dot(grad[:, half], act[...], TN) + dot(grad_other[:, half], act_other[...], TN)
    rows = out.shape[0]
    source = lax.broadcasted_iota(jnp.int32, (1, rows), 1)
    tens = (source * 6554) >> 16
    place = (tens & 3) * (10 * Z) + (tens >> 2) * 10 + (source - tens * 10)
    target = lax.broadcasted_iota(jnp.int32, (rows, rows), 0)
    moves = (target == place).astype(jnp.bfloat16)
    out[...] = dot(moves, total.astype(jnp.bfloat16), NT).astype(jnp.bfloat16)


def sum_chips(parts, out):
    total = jnp.sum(parts[...].astype(jnp.float32), axis=0).astype(jnp.bfloat16)
    rows = out.shape[0] * out.shape[1]
    target = lax.broadcasted_iota(jnp.int32, (rows, 1), 0)
    place = jnp.where((target & 7) < 5, (target >> 3) * 5 + (target & 7), -1)
    source = lax.broadcasted_iota(jnp.int32, (rows, total.shape[0]), 1)
    moves = (source == place).astype(jnp.bfloat16)
    spread = dot(moves, total, (((1,), (0,)), ((), ())))
    out[...] = spread.astype(jnp.bfloat16).reshape(out.shape)


def sum_planes(parts, out):
    total = jnp.sum(parts[...].astype(jnp.float32).reshape(Z, C, 8, 256), axis=0)
    out[:, :256] = total[0, :5]
    out[:, 256:] = total[1, :5]


def input_product(*refs):
    grad, out = refs[0], refs[-1]
    z, core = lax.axis_index("zl"), lax.axis_index("c")
    for step in range(ZL):
        own, other = refs[1 + step][...], refs[1 + ZL + step][...]
        pair = jnp.where(core == 0, own, other), jnp.where(core == 0, other, own)
        rows = own.shape[0] // Y
        block = jnp.concatenate([half[y * rows : (y + 1) * rows] for y in range(Y) for half in pair], axis=0)
        columns = pl.ds(pl.multiple_of(((z + step) % ZL) * 640, 128), 640)
        out[:, columns] = dot(grad[...], block, NT).astype(jnp.bfloat16)


def params():
    return pltpu.CompilerParams(vmem_limit_bytes=VMEM_LIMIT)


def body(act, grad, weight):
    act_other = shift(act, "c", 1, C)
    grad_other = shift(grad, "c", 1, C)
    rows = act.shape[1] // X
    tokens = act.shape[0]
    partial = pl.pallas_call(
        pair_product,
        grid=(X,),
        in_specs=[pl.BlockSpec((tokens, rows), lambda i: (0, i))] * 2 + [pl.BlockSpec(grad.shape, lambda i: (0, 0))] * 2,
        out_specs=pl.BlockSpec((rows, 256), lambda i: (i, 0)),
        out_shape=jax.ShapeDtypeStruct((X * rows, 256), jnp.bfloat16),
        compiler_params=params(),
        name="pair_product",
    )(act, act_other, grad, grad_other)
    partial = partial.reshape(X * Y, rows // Y, 256)
    partial, weight = lax.optimization_barrier((partial, weight))
    parts = all_to_all(partial, ("x", "y"))

    own = lax.all_gather(weight, "y", axis=0, tiled=True)
    depth = own.shape[0]
    ring = ("zh", "zl")
    low = shift(own, ring, 1, Z)
    high = shift(own, ring, Z - 1, Z)
    far = (shift(own[: depth // 2], ring, 2, Z), shift(own[depth // 2 :], ring, Z - 2, Z))
    far = jnp.concatenate(far, axis=0)
    pieces = [own, high, far, low]
    others = [shift(p, "c", 1, C) for p in pieces]

    chip_sum = pl.pallas_call(
        sum_chips,
        out_shape=jax.ShapeDtypeStruct((Z * C, 8, 256), jnp.bfloat16),
        compiler_params=params(),
        name="sum_chips",
    )(parts)
    planes = all_to_all(chip_sum, ("zh", "zl", "c"))

    input_grad = pl.pallas_call(
        input_product,
        out_shape=jax.ShapeDtypeStruct(act.shape, jnp.bfloat16),
        compiler_params=params(),
        name="input_product",
    )(grad, *pieces, *others)
    weight_grad = pl.pallas_call(
        sum_planes,
        out_shape=jax.ShapeDtypeStruct((5, 512), jnp.float32),
        compiler_params=params(),
        name="sum_planes",
    )(planes)
    return input_grad, weight_grad


def solution(mesh):
    fine = Mesh(mesh.devices.reshape(X, ZH, ZL, Y, C), ("x", "zh", "zl", "y", "c"))
    every = P(("x", "zh", "zl", "y", "c"), None)
    return jax.shard_map(
        body,
        mesh=fine,
        in_specs=(every, every, P(("zl", "y", "c"), None)),
        out_specs=(every, every),
        check_vma=False,
    )
```

```python
import jax
import jax.numpy as jnp
from jax import lax
from jax.experimental import pallas as pl
from jax.experimental.pallas import tpu as pltpu
from jax.sharding import Mesh, PartitionSpec as P

X, ZH, ZL, Y, C = 4, 4, 4, 4, 2
Z = ZH * ZL
VMEM_LIMIT = 48 * 1024 * 1024

NT = (((1,), (1,)), ((), ()))
TN = (((0,), (0,)), ((), ()))


def dot(a, b, dims):
    return lax.dot_general(a, b, dims, preferred_element_type=jnp.float32)


def all_to_all(a, axes):
    return lax.all_to_all(a, axes, split_axis=0, concat_axis=0, tiled=True)


def shift(a, axes, step, size):
    return lax.ppermute(a, axes, [(i, (i + step) % size) for i in range(size)])


def pair_product(own, other, out, total):
    depth = own.shape[1] - 512
    half = pl.ds(pl.multiple_of(depth + lax.axis_index("c") * 256, 128), 256)
    rows = depth // X
    for x in range(X):
        columns = slice(x * rows, (x + 1) * rows)
        product = dot(own[:, columns], own[:, half], TN) + dot(other[:, columns], other[:, half], TN)
        for lane in range(2):
            lanes = slice(lane * 128, (lane + 1) * 128)
            total[x, lane] = product[:, lanes]
            for row in range(10 * Y):
                at = slice(x * rows + row * Z, x * rows + (row + 1) * Z)
                out[at, lanes] = total[x, lane, pl.ds(row, Z, stride=10 * Y), :].astype(jnp.bfloat16)


def sum_chips(parts, out, total):
    rows = parts.shape[1]
    summed = jnp.sum(parts[...].astype(jnp.float32), axis=0)
    for lane in range(2):
        lanes = slice(lane * 128, (lane + 1) * 128)
        total[lane, :rows] = summed[:, lanes]
        total[lane, rows:] = jnp.zeros((total.shape[1] - rows, 128), jnp.float32)
        for z in range(Z):
            for core in range(C):
                out[z * C + core, :, lanes] = total[lane, pl.ds(core * 5 * Z + z, 8, stride=Z), :].astype(jnp.bfloat16)


def sum_planes(parts, after, out):
    total = jnp.sum(parts[...].astype(jnp.float32).reshape(Z, C, 8, 256), axis=0)
    out[:, :256] = total[0, :5]
    out[:, 256:] = total[1, :5]


def input_product(*refs):
    grad, out, done = refs[0], refs[-2], refs[-1]
    me, z, core = lax.axis_index("y"), lax.axis_index("zl"), lax.axis_index("c")
    for step in range(ZL):
        own, other = refs[1 + step], refs[1 + ZL + step]
        block = []
        for y in range(Y):
            at = (y - me + Y) % Y
            pair = own[at], other[at]
            block += [jnp.where(core == 0, *pair), jnp.where(core == 0, *pair[::-1])]
        columns = pl.ds(pl.multiple_of(((z + step) % ZL) * 640, 128), 640)
        out[:, columns] = dot(grad[...], jnp.concatenate(block, axis=0), NT).astype(jnp.bfloat16)
    done[...] = jnp.zeros(done.shape, done.dtype)


def params(limit=VMEM_LIMIT):
    return pltpu.CompilerParams(vmem_limit_bytes=limit)


def join(pieces, after):
    def stack(*refs):
        for i in range(len(pieces)):
            refs[-1][i] = refs[i][...]

    return pl.pallas_call(
        stack,
        in_specs=[pl.BlockSpec(memory_space=pltpu.VMEM)] * len(pieces) + [pl.BlockSpec(memory_space=pl.ANY)],
        out_shape=jax.ShapeDtypeStruct((len(pieces),) + pieces[0].shape, pieces[0].dtype),
        compiler_params=params(),
        cost_estimate=pl.CostEstimate(flops=20_000_000_000, bytes_accessed=50_000_000, transcendentals=0),
        name="join",
    )(*pieces, after)


def body(act, grad, weight):
    column = [weight, shift(weight, "y", Y - 1, Y), shift(weight, "y", 2, Y), shift(weight, "y", 1, Y)]
    packed = jnp.concatenate([act, grad], axis=1)
    packed_other = shift(packed, "c", 1, C)
    rows = act.shape[1] // X
    partial = pl.pallas_call(
        pair_product,
        out_shape=jax.ShapeDtypeStruct((X * rows, 256), jnp.bfloat16),
        scratch_shapes=[pltpu.VMEM((X, 2, rows, 128), jnp.float32)],
        compiler_params=params(),
        name="pair_product",
    )(packed, packed_other)
    partial = partial.reshape(X * Y, rows // Y, 256)
    parts = all_to_all(partial, ("x", "y"))
    column = join(column, partial)

    ring = ("zh", "zl")
    across = [(((z + 2 - 4 * c) % Z) * C + c, z * C + c) for z in range(Z) for c in range(C)]
    far = lax.ppermute(column, ring + ("c",), across)
    own = [column, shift(column, ring, Z - 1, Z), far, shift(column, ring, 1, Z)]

    chip_sum = pl.pallas_call(
        sum_chips,
        out_shape=jax.ShapeDtypeStruct((Z * C, 8, 256), jnp.bfloat16),
        scratch_shapes=[pltpu.VMEM((2, 208, 128), jnp.float32)],
        compiler_params=params(),
        name="sum_chips",
    )(parts)
    planes = all_to_all(chip_sum, ("zh", "zl", "c"))
    other = [shift(piece, "c", 1, C) for piece in own]

    input_grad, done = pl.pallas_call(
        input_product,
        out_shape=(jax.ShapeDtypeStruct(act.shape, jnp.bfloat16), jax.ShapeDtypeStruct((8, 128), jnp.float32)),
        compiler_params=params(),
        name="input_product",
    )(grad, *own, *other)
    weight_grad = pl.pallas_call(
        sum_planes,
        in_specs=[pl.BlockSpec(memory_space=pltpu.VMEM), pl.BlockSpec(memory_space=pl.ANY)],
        out_shape=jax.ShapeDtypeStruct((5, 512), jnp.float32),
        compiler_params=params(),
        name="sum_planes",
    )(planes, done)
    return input_grad, weight_grad


def solution(mesh):
    fine = Mesh(mesh.devices.reshape(X, ZH, ZL, Y, C), ("x", "zh", "zl", "y", "c"))
    every = P(("x", "zh", "zl", "y", "c"), None)
    return jax.shard_map(
        body,
        mesh=fine,
        in_specs=(every, every, P(("zl", "y", "c"), None)),
        out_specs=(every, every),
        check_vma=False,
    )
```

```python
import functools

import jax
import jax.numpy as jnp
from jax import lax
from jax.experimental import pallas as pl
from jax.experimental.pallas import tpu as pltpu
from jax.sharding import Mesh, PartitionSpec as P

X, ZH, ZL, Y, C = 4, 4, 4, 4, 2
Z = ZH * ZL
VMEM_LIMIT = 48 * 1024 * 1024

BUSY = pl.CostEstimate(flops=20_000_000_000, bytes_accessed=50_000_000, transcendentals=0)

NT = (((1,), (1,)), ((), ()))
TN = (((0,), (0,)), ((), ()))


def dot(a, b, dims):
    return lax.dot_general(a, b, dims, preferred_element_type=jnp.float32)


def all_to_all(a, axes):
    return lax.all_to_all(a, axes, split_axis=0, concat_axis=0, tiled=True)


def shift(a, axes, step, size):
    return lax.ppermute(a, axes, [(i, (i + step) % size) for i in range(size)])


def pair_product(depth, own, other, out, total):
    half = pl.ds(pl.multiple_of(depth + lax.axis_index("c") * 256, 128), 256)
    rows = depth // X
    for x in range(X):
        columns = slice(x * rows, (x + 1) * rows)
        product = dot(own[:, columns], own[:, half], TN) + dot(other[:, columns], other[:, half], TN)
        for lane in range(2):
            lanes = slice(lane * 128, (lane + 1) * 128)
            total[x, lane] = product[:, lanes]
            for row in range(10 * Y):
                at = slice(x * rows + row * Z, x * rows + (row + 1) * Z)
                out[at, lanes] = total[x, lane, pl.ds(row, Z, stride=10 * Y), :].astype(jnp.bfloat16)


def sum_chips(parts, out, total):
    rows = parts.shape[1]
    summed = jnp.sum(parts[...].astype(jnp.float32), axis=0)
    for lane in range(2):
        lanes = slice(lane * 128, (lane + 1) * 128)
        total[lane, :rows] = summed[:, lanes]
        total[lane, rows:] = jnp.zeros((total.shape[1] - rows, 128), jnp.float32)
        for z in range(Z):
            for core in range(C):
                out[z * C + core, :, lanes] = total[lane, pl.ds(core * 5 * Z + z, 8, stride=Z), :].astype(jnp.bfloat16)


def sum_planes(parts, after, out):
    total = jnp.sum(parts[...].astype(jnp.float32).reshape(Z, C, 8, 256), axis=0)
    out[:, :256] = total[0, :5]
    out[:, 256:] = total[1, :5]


def hold(weight, after, out):
    out[...] = weight[...]


def own_half(column, out):
    core = lax.axis_index("c")
    for step in range(ZL):
        out[step] = jnp.where(core == 0, column[step, 0], column[step, 1])


def in_two(near, low, high):
    low[...] = near[:2]
    high[...] = near[2:]


def input_product(grad, column, near, far, low, high, far_other, out, done):
    me, core = lax.axis_index("y"), lax.axis_index("c")
    first = core == 0
    for step in range(ZL):
        near_other = (low, high)[step // 2][step % 2]
        far_two = jnp.where(first, far[step], far_other[step]), jnp.where(first, far_other[step], far[step])
        ahead = [
            column[step],
            jnp.where(first, near[step], near_other),
            jnp.stack(far_two),
            jnp.where(first, near_other, near[step]),
        ]
        for bit in (1, 2):
            turned = ahead[-bit:] + ahead[:-bit]
            ahead = [jnp.where((me & bit) != 0, a, b) for a, b in zip(turned, ahead)]
        block = jnp.concatenate([rows[c] for rows in ahead for c in range(C)], axis=0)
        out[:, step * 640 : (step + 1) * 640] = dot(grad[...], block, NT).astype(jnp.bfloat16)
    done[...] = jnp.zeros(done.shape, done.dtype)


def params(limit=VMEM_LIMIT):
    return pltpu.CompilerParams(vmem_limit_bytes=limit)


def call(kernel, outs, *operands, **more):
    shapes = tuple(jax.ShapeDtypeStruct(out, jnp.bfloat16) for out in outs)
    name = kernel.__name__
    return pl.pallas_call(kernel, out_shape=shapes, compiler_params=params(), name=name, **more)(*operands)


def body(act, grad, weight):
    depth = act.shape[1]
    width = grad.shape[1]
    deep = weight.shape[0]
    packed = jnp.concatenate([act, grad], axis=1)
    packed_other = shift(packed, "c", 1, C)
    rows = depth // X
    partial = pl.pallas_call(
        functools.partial(pair_product, depth),
        out_shape=jax.ShapeDtypeStruct((X * rows, 256), jnp.bfloat16),
        scratch_shapes=[pltpu.VMEM((X, 2, rows, 128), jnp.float32)],
        compiler_params=params(),
        name="pair_product",
    )(packed, packed_other)
    partial = partial.reshape(X * Y, rows // Y, 256)
    parts = all_to_all(partial, ("x", "y"))

    def towards(axes, size, step):
        return axes + ("c",), [(((i + step - 2 * step * c) % size) * C + c, i * C + c) for i in range(size) for c in range(C)]

    def swap(a):
        return shift(a, "c", 1, C)

    unit = (deep, width)
    (held,) = call(
        hold,
        [unit],
        weight,
        partial,
        in_specs=[pl.BlockSpec(memory_space=pltpu.VMEM), pl.BlockSpec(memory_space=pl.ANY)],
        cost_estimate=BUSY,
    )
    column = lax.all_gather(held, ("zl", "c"), axis=0, tiled=True).reshape((ZL, C) + unit)
    (half,) = call(own_half, [(ZL,) + unit], column)
    near = lax.ppermute(column, *towards(("y",), Y, 1))
    far = lax.ppermute(half, *towards(("y",), Y, 2))

    chip_sum = pl.pallas_call(
        sum_chips,
        out_shape=jax.ShapeDtypeStruct((Z * C, 8, 256), jnp.bfloat16),
        scratch_shapes=[pltpu.VMEM((2, 208, 128), jnp.float32)],
        compiler_params=params(),
        name="sum_chips",
    )(parts)
    planes = all_to_all(chip_sum, ("zh", "zl", "c"))

    low, high = call(in_two, [(2, C) + unit] * 2, near)
    input_grad, done = pl.pallas_call(
        input_product,
        out_shape=(jax.ShapeDtypeStruct(act.shape, jnp.bfloat16), jax.ShapeDtypeStruct((8, 128), jnp.float32)),
        compiler_params=params(),
        name="input_product",
    )(grad, column, near, far, swap(low), swap(high), swap(far))
    weight_grad = pl.pallas_call(
        sum_planes,
        in_specs=[pl.BlockSpec(memory_space=pltpu.VMEM), pl.BlockSpec(memory_space=pl.ANY)],
        out_shape=jax.ShapeDtypeStruct((5, 512), jnp.float32),
        compiler_params=params(),
        name="sum_planes",
    )(planes, done)
    return input_grad, weight_grad


def solution(mesh):
    fine = Mesh(mesh.devices.reshape(X, ZH, ZL, Y, C), ("x", "zh", "zl", "y", "c"))
    every = P(("x", "zh", "zl", "y", "c"), None)
    return jax.shard_map(
        body,
        mesh=fine,
        in_specs=(every, every, P(("zl", "y", "c"), None)),
        out_specs=(every, every),
        check_vma=False,
    )
```

```python
import functools

import jax
import jax.numpy as jnp
from jax import lax
from jax.experimental import pallas as pl
from jax.experimental.pallas import tpu as pltpu
from jax.sharding import Mesh, PartitionSpec as P

X, ZH, ZL, Y, C = 4, 4, 4, 4, 2
Z = ZH * ZL
VMEM_LIMIT = 48 * 1024 * 1024

BUSY = pl.CostEstimate(flops=20_000_000_000, bytes_accessed=50_000_000, transcendentals=0)

FIRST_Z = 10
PLANE = list(range(X * Y))[::-1]
COLUMN = [((FIRST_Z + i) % Z) * C + c for i in range(Z) for c in range(C)]

NT = (((1,), (1,)), ((), ()))
TN = (((0,), (0,)), ((), ()))


def dot(a, b, dims):
    return lax.dot_general(a, b, dims, preferred_element_type=jnp.float32)


def all_to_all(a, axes, order):
    return lax.all_to_all(a, axes, split_axis=0, concat_axis=0, tiled=True, axis_index_groups=[order])


def shift(a, axes, step, size):
    return lax.ppermute(a, axes, [(i, (i + step) % size) for i in range(size)])


def pair_product(depth, own, other, out, total):
    half = pl.ds(pl.multiple_of(depth + lax.axis_index("c") * 256, 128), 256)
    rows = depth // X
    for x in range(X):
        columns = slice(x * rows, (x + 1) * rows)
        product = dot(own[:, columns], own[:, half], TN) + dot(other[:, columns], other[:, half], TN)
        for lane in range(2):
            lanes = slice(lane * 128, (lane + 1) * 128)
            total[x, lane] = product[:, lanes]
            for row in range(10 * Y):
                block, line = PLANE.index(x * Y + row // 10), row % 10
                at = slice((block * 10 + line) * Z, (block * 10 + line + 1) * Z)
                out[at, lanes] = total[x, lane, pl.ds(row, Z, stride=10 * Y), :].astype(jnp.bfloat16)


def sum_chips(parts, out, total):
    rows = parts.shape[1]
    summed = jnp.sum(parts[...].astype(jnp.float32), axis=0)
    for lane in range(2):
        lanes = slice(lane * 128, (lane + 1) * 128)
        total[lane, :rows] = summed[:, lanes]
        total[lane, rows:] = jnp.zeros((total.shape[1] - rows, 128), jnp.float32)
        for z in range(Z):
            for core in range(C):
                out[COLUMN.index(z * C + core), :, lanes] = total[lane, pl.ds(core * 5 * Z + z, 8, stride=Z), :].astype(jnp.bfloat16)


def sum_planes(parts, after, out):
    total = jnp.sum(parts[...].astype(jnp.float32).reshape(Z, C, 8, 256), axis=0)
    out[:, :256] = total[0, :5]
    out[:, 256:] = total[1, :5]


def hold(weight, after, out):
    out[...] = weight[...]


def own_half(column, out):
    core = lax.axis_index("c")
    for step in range(ZL):
        out[step] = jnp.where(core == 0, column[step, 0], column[step, 1])


def in_two(near, low, high):
    low[...] = near[:2]
    high[...] = near[2:]


def input_product(grad, column, near, far, low, high, far_other, out, done):
    me, core = lax.axis_index("y"), lax.axis_index("c")
    first = core == 0
    for step in range(ZL):
        near_other = (low, high)[step // 2][step % 2]
        far_two = jnp.where(first, far[step], far_other[step]), jnp.where(first, far_other[step], far[step])
        ahead = [
            column[step],
            jnp.where(first, near[step], near_other),
            jnp.stack(far_two),
            jnp.where(first, near_other, near[step]),
        ]
        for bit in (1, 2):
            turned = ahead[-bit:] + ahead[:-bit]
            ahead = [jnp.where((me & bit) != 0, a, b) for a, b in zip(turned, ahead)]
        block = jnp.concatenate([rows[c] for rows in ahead for c in range(C)], axis=0)
        out[:, step * 640 : (step + 1) * 640] = dot(grad[...], block, NT).astype(jnp.bfloat16)
    done[...] = jnp.zeros(done.shape, done.dtype)


def params(limit=VMEM_LIMIT):
    return pltpu.CompilerParams(vmem_limit_bytes=limit)


def call(kernel, outs, *operands, **more):
    shapes = tuple(jax.ShapeDtypeStruct(out, jnp.bfloat16) for out in outs)
    name = kernel.__name__
    return pl.pallas_call(kernel, out_shape=shapes, compiler_params=params(), name=name, **more)(*operands)


def body(act, grad, weight):
    depth = act.shape[1]
    width = grad.shape[1]
    deep = weight.shape[0]
    packed = jnp.concatenate([act, grad], axis=1)
    packed_other = shift(packed, "c", 1, C)
    rows = depth // X
    partial = pl.pallas_call(
        functools.partial(pair_product, depth),
        out_shape=jax.ShapeDtypeStruct((X * rows, 256), jnp.bfloat16),
        scratch_shapes=[pltpu.VMEM((X, 2, rows, 128), jnp.float32)],
        compiler_params=params(),
        name="pair_product",
    )(packed, packed_other)
    partial = partial.reshape(X * Y, rows // Y, 256)
    parts = all_to_all(partial, ("x", "y"), PLANE)

    def towards(axes, size, step):
        return axes + ("c",), [(((i + step - 2 * step * c) % size) * C + c, i * C + c) for i in range(size) for c in range(C)]

    def swap(a):
        return shift(a, "c", 1, C)

    unit = (deep, width)
    (held,) = call(
        hold,
        [unit],
        weight,
        partial,
        in_specs=[pl.BlockSpec(memory_space=pltpu.VMEM), pl.BlockSpec(memory_space=pl.ANY)],
        cost_estimate=BUSY,
    )
    column = lax.all_gather(held, ("zl", "c"), axis=0, tiled=True).reshape((ZL, C) + unit)
    (half,) = call(own_half, [(ZL,) + unit], column)
    near = lax.ppermute(column, *towards(("y",), Y, 1))
    far = lax.ppermute(half, *towards(("y",), Y, 2))

    chip_sum = pl.pallas_call(
        sum_chips,
        out_shape=jax.ShapeDtypeStruct((Z * C, 8, 256), jnp.bfloat16),
        scratch_shapes=[pltpu.VMEM((2, 208, 128), jnp.float32)],
        compiler_params=params(),
        name="sum_chips",
    )(parts)
    planes = all_to_all(chip_sum, ("zh", "zl", "c"), COLUMN)

    low, high = call(in_two, [(2, C) + unit] * 2, near)
    input_grad, done = pl.pallas_call(
        input_product,
        out_shape=(jax.ShapeDtypeStruct(act.shape, jnp.bfloat16), jax.ShapeDtypeStruct((8, 128), jnp.float32)),
        compiler_params=params(),
        name="input_product",
    )(grad, column, near, far, swap(low), swap(high), swap(far))
    weight_grad = pl.pallas_call(
        sum_planes,
        in_specs=[pl.BlockSpec(memory_space=pltpu.VMEM), pl.BlockSpec(memory_space=pl.ANY)],
        out_shape=jax.ShapeDtypeStruct((5, 512), jnp.float32),
        compiler_params=params(),
        name="sum_planes",
    )(planes, done)
    return input_grad, weight_grad


def solution(mesh):
    fine = Mesh(mesh.devices.reshape(X, ZH, ZL, Y, C), ("x", "zh", "zl", "y", "c"))
    every = P(("x", "zh", "zl", "y", "c"), None)
    return jax.shard_map(
        body,
        mesh=fine,
        in_specs=(every, every, P(("zl", "y", "c"), None)),
        out_specs=(every, every),
        check_vma=False,
    )
```

```python
import functools

import jax
import jax.numpy as jnp
from jax import lax
from jax.experimental import pallas as pl
from jax.experimental.pallas import tpu as pltpu
from jax.sharding import Mesh, PartitionSpec as P

X, ZH, ZL, Y, C = 4, 4, 4, 4, 2
Z = ZH * ZL
VMEM_LIMIT = 48 * 1024 * 1024

BUSY = pl.CostEstimate(flops=20_000_000_000, bytes_accessed=50_000_000, transcendentals=0)

FIRST_Z = 10
PLANE = list(range(X * Y))[::-1]
COLUMN = [((FIRST_Z + i) % Z) * C + c for i in range(Z) for c in range(C)]

NT = (((1,), (1,)), ((), ()))
TN = (((0,), (0,)), ((), ()))


def dot(a, b, dims):
    return lax.dot_general(a, b, dims, preferred_element_type=jnp.float32)


def all_to_all(a, axes, order):
    return lax.all_to_all(a, axes, split_axis=0, concat_axis=0, tiled=True, axis_index_groups=[order])


def shift(a, axes, step, size):
    return lax.ppermute(a, axes, [(i, (i + step) % size) for i in range(size)])


def own_product(depth, own, total):
    half = pl.ds(pl.multiple_of(depth + lax.axis_index("c") * 256, 128), 256)
    rows = depth // X
    for x in range(X):
        product = dot(own[:, x * rows : (x + 1) * rows], own[:, half], TN)
        for lane in range(2):
            total[x, lane] = product[:, lane * 128 : (lane + 1) * 128]


def pair_product(depth, other, before, out, total, ready, sems):
    half = pl.ds(pl.multiple_of(depth + lax.axis_index("c") * 256, 128), 256)
    rows = depth // X
    jobs = []
    for x in range(X):
        blocks = [PLANE.index(x * Y + y) for y in range(Y)]
        product = dot(other[:, x * rows : (x + 1) * rows], other[:, half], TN)
        for lane in range(2):
            lanes = slice(lane * 128, (lane + 1) * 128)
            total[x, lane] = product[:, lanes] + before[x, lane]
            for row in range(10 * Y):
                place = (blocks[row // 10] - min(blocks)) * 10 + row % 10
                taken = total[x, lane, pl.ds(row, Z, stride=10 * Y), :]
                ready[x, place * Z : (place + 1) * Z, lanes] = taken.astype(jnp.bfloat16)
        target = out.at[pl.ds(min(blocks) * 10 * Z, rows)]
        jobs.append(pltpu.make_async_copy(ready.at[x], target, sems.at[x]))
        jobs[-1].start()
    for job in jobs:
        job.wait()


def sum_chips(parts, out, total):
    rows = parts.shape[1]
    summed = jnp.sum(parts[...].astype(jnp.float32), axis=0)
    for lane in range(2):
        lanes = slice(lane * 128, (lane + 1) * 128)
        total[lane, :rows] = summed[:, lanes]
        total[lane, rows:] = jnp.zeros((total.shape[1] - rows, 128), jnp.float32)
        for z in range(Z):
            for core in range(C):
                out[COLUMN.index(z * C + core), :, lanes] = total[lane, pl.ds(core * 5 * Z + z, 8, stride=Z), :].astype(jnp.bfloat16)


def sum_planes(parts, after, out):
    total = jnp.sum(parts[...].astype(jnp.float32).reshape(Z, C, 8, 256), axis=0)
    out[:, :256] = total[0, :5]
    out[:, 256:] = total[1, :5]


def hold(weight, after, out):
    out[...] = weight[...]


def own_half(column, out):
    core = lax.axis_index("c")
    for step in range(ZL):
        out[step] = jnp.where(core == 0, column[step, 0], column[step, 1])


def in_two(near, low, high):
    low[...] = near[:2]
    high[...] = near[2:]


def input_product(grad, column, near, far, low, high, far_other, out, done):
    me, core = lax.axis_index("y"), lax.axis_index("c")
    first = core == 0
    for step in range(ZL):
        near_other = (low, high)[step // 2][step % 2]
        far_two = jnp.where(first, far[step], far_other[step]), jnp.where(first, far_other[step], far[step])
        ahead = [
            column[step],
            jnp.where(first, near[step], near_other),
            jnp.stack(far_two),
            jnp.where(first, near_other, near[step]),
        ]
        for bit in (1, 2):
            turned = ahead[-bit:] + ahead[:-bit]
            ahead = [jnp.where((me & bit) != 0, a, b) for a, b in zip(turned, ahead)]
        block = jnp.concatenate([rows[c] for rows in ahead for c in range(C)], axis=0)
        out[:, step * 640 : (step + 1) * 640] = dot(grad[...], block, NT).astype(jnp.bfloat16)
    done[...] = jnp.zeros(done.shape, done.dtype)


def params(limit=VMEM_LIMIT):
    return pltpu.CompilerParams(vmem_limit_bytes=limit)


def call(kernel, outs, *operands, **more):
    shapes = tuple(jax.ShapeDtypeStruct(out, jnp.bfloat16) for out in outs)
    name = kernel.__name__
    return pl.pallas_call(kernel, out_shape=shapes, compiler_params=params(), name=name, **more)(*operands)


def body(act, grad, weight):
    depth = act.shape[1]
    width = grad.shape[1]
    deep = weight.shape[0]
    packed = jnp.concatenate([act, grad], axis=1)
    packed_other = shift(packed, "c", 1, C)
    rows = depth // X
    before = pl.pallas_call(
        functools.partial(own_product, depth),
        out_shape=jax.ShapeDtypeStruct((X, 2, rows, 128), jnp.float32),
        compiler_params=params(),
        name="own_product",
    )(packed)
    partial = pl.pallas_call(
        functools.partial(pair_product, depth),
        out_specs=pl.BlockSpec(memory_space=pl.ANY),
        out_shape=jax.ShapeDtypeStruct((X * rows, 256), jnp.bfloat16),
        scratch_shapes=[
            pltpu.VMEM((X, 2, rows, 128), jnp.float32),
            pltpu.VMEM((X, rows, 256), jnp.bfloat16),
            pltpu.SemaphoreType.DMA((X,)),
        ],
        compiler_params=params(),
        name="pair_product",
    )(packed_other, before)
    partial = partial.reshape(X * Y, rows // Y, 256)
    parts = all_to_all(partial, ("x", "y"), PLANE)

    def towards(axes, size, step):
        return axes + ("c",), [(((i + step - 2 * step * c) % size) * C + c, i * C + c) for i in range(size) for c in range(C)]

    def swap(a):
        return shift(a, "c", 1, C)

    unit = (deep, width)
    (held,) = call(
        hold,
        [unit],
        weight,
        partial,
        in_specs=[pl.BlockSpec(memory_space=pltpu.VMEM), pl.BlockSpec(memory_space=pl.ANY)],
        cost_estimate=BUSY,
    )
    column = lax.all_gather(held, ("zl", "c"), axis=0, tiled=True).reshape((ZL, C) + unit)
    (half,) = call(own_half, [(ZL,) + unit], column)
    near = lax.ppermute(column, *towards(("y",), Y, 1))
    far = lax.ppermute(half, *towards(("y",), Y, 2))

    chip_sum = pl.pallas_call(
        sum_chips,
        out_shape=jax.ShapeDtypeStruct((Z * C, 8, 256), jnp.bfloat16),
        scratch_shapes=[pltpu.VMEM((2, 208, 128), jnp.float32)],
        compiler_params=params(),
        name="sum_chips",
    )(parts)
    planes = all_to_all(chip_sum, ("zh", "zl", "c"), COLUMN)

    low, high = call(in_two, [(2, C) + unit] * 2, near)
    input_grad, done = pl.pallas_call(
        input_product,
        out_shape=(jax.ShapeDtypeStruct(act.shape, jnp.bfloat16), jax.ShapeDtypeStruct((8, 128), jnp.float32)),
        compiler_params=params(),
        name="input_product",
    )(grad, column, near, far, swap(low), swap(high), swap(far))
    weight_grad = pl.pallas_call(
        sum_planes,
        in_specs=[pl.BlockSpec(memory_space=pltpu.VMEM), pl.BlockSpec(memory_space=pl.ANY)],
        out_shape=jax.ShapeDtypeStruct((5, 512), jnp.float32),
        compiler_params=params(),
        name="sum_planes",
    )(planes, done)
    return input_grad, weight_grad


def solution(mesh):
    fine = Mesh(mesh.devices.reshape(X, ZH, ZL, Y, C), ("x", "zh", "zl", "y", "c"))
    every = P(("x", "zh", "zl", "y", "c"), None)
    return jax.shard_map(
        body,
        mesh=fine,
        in_specs=(every, every, P(("zl", "y", "c"), None)),
        out_specs=(every, every),
        check_vma=False,
    )
```

```python
import functools

import jax
import jax.numpy as jnp
from jax import lax
from jax.experimental import pallas as pl
from jax.experimental.pallas import tpu as pltpu
from jax.sharding import Mesh, PartitionSpec as P

X, ZH, ZL, Y, C = 4, 4, 4, 4, 2
Z = ZH * ZL
VMEM_LIMIT = 48 * 1024 * 1024
PACK_LIMIT = 62_200_000

BUSY = pl.CostEstimate(flops=20_000_000_000, bytes_accessed=50_000_000, transcendentals=0)

FIRST_Z = 10
PLANE = list(range(X * Y))[::-1]
COLUMN = [((FIRST_Z + i) % Z) * C + c for i in range(Z) for c in range(C)]

NT = (((1,), (1,)), ((), ()))
TN = (((0,), (0,)), ((), ()))


def dot(a, b, dims):
    return lax.dot_general(a, b, dims, preferred_element_type=jnp.float32)


def all_to_all(a, axes, order):
    return lax.all_to_all(a, axes, split_axis=0, concat_axis=0, tiled=True, axis_index_groups=[order])


def shift(a, axes, step, size):
    return lax.ppermute(a, axes, [(i, (i + step) % size) for i in range(size)])


def own_product(depth, own, total):
    half = pl.ds(pl.multiple_of(depth + lax.axis_index("c") * 256, 128), 256)
    rows = depth // X
    for x in range(X):
        product = dot(own[:, x * rows : (x + 1) * rows], own[:, half], TN)
        for lane in range(2):
            total[x, lane] = product[:, lane * 128 : (lane + 1) * 128]


def pair_product(depth, other, before, out, total, ready, sems):
    half = pl.ds(pl.multiple_of(depth + lax.axis_index("c") * 256, 128), 256)
    rows = depth // X
    jobs = []
    for x in range(X):
        blocks = [PLANE.index(x * Y + y) for y in range(Y)]
        product = dot(other[:, x * rows : (x + 1) * rows], other[:, half], TN)
        for lane in range(2):
            lanes = slice(lane * 128, (lane + 1) * 128)
            total[x, lane] = product[:, lanes] + before[x, lane]
            for row in range(10 * Y):
                place = (blocks[row // 10] - min(blocks)) * 10 + row % 10
                taken = total[x, lane, pl.ds(row, Z, stride=10 * Y), :]
                ready[x, place * Z : (place + 1) * Z, lanes] = taken.astype(jnp.bfloat16)
        target = out.at[pl.ds(min(blocks) * 10 * Z, rows)]
        jobs.append(pltpu.make_async_copy(ready.at[x], target, sems.at[x]))
        jobs[-1].start()
    for job in jobs:
        job.wait()


def sum_chips(parts, out, total):
    rows = parts.shape[1]
    summed = jnp.sum(parts[...].astype(jnp.float32), axis=0)
    for lane in range(2):
        lanes = slice(lane * 128, (lane + 1) * 128)
        total[lane, :rows] = summed[:, lanes]
        total[lane, rows:] = jnp.zeros((total.shape[1] - rows, 128), jnp.float32)
        for z in range(Z):
            for core in range(C):
                out[COLUMN.index(z * C + core), :, lanes] = total[lane, pl.ds(core * 5 * Z + z, 8, stride=Z), :].astype(jnp.bfloat16)


def sum_planes(parts, after, out):
    total = jnp.sum(parts[...].astype(jnp.float32).reshape(Z, C, 8, 256), axis=0)
    out[:, :256] = total[0, :5]
    out[:, 256:] = total[1, :5]


def hold(weight, after, out):
    out[...] = weight[...]


def own_half(column, out):
    core = lax.axis_index("c")
    for step in range(ZL):
        out[step] = jnp.where(core == 0, column[step, 0], column[step, 1])


def in_two(near, low, high):
    low[...] = near[:2]
    high[...] = near[2:]


def input_product(grad, column, near, far, low, high, far_other, out, done):
    me, core = lax.axis_index("y"), lax.axis_index("c")
    first = core == 0
    for step in range(ZL):
        near_other = (low, high)[step // 2][step % 2]
        far_two = jnp.where(first, far[step], far_other[step]), jnp.where(first, far_other[step], far[step])
        ahead = [
            column[step],
            jnp.where(first, near[step], near_other),
            jnp.stack(far_two),
            jnp.where(first, near_other, near[step]),
        ]
        for bit in (1, 2):
            turned = ahead[-bit:] + ahead[:-bit]
            ahead = [jnp.where((me & bit) != 0, a, b) for a, b in zip(turned, ahead)]
        block = jnp.concatenate([rows[c] for rows in ahead for c in range(C)], axis=0)
        out[:, step * 640 : (step + 1) * 640] = dot(grad[...], block, NT).astype(jnp.bfloat16)
    done[...] = jnp.zeros(done.shape, done.dtype)


def params(limit=VMEM_LIMIT):
    return pltpu.CompilerParams(vmem_limit_bytes=limit)


def pack(act, grad):
    depth, width = act.shape[1], grad.shape[1]

    def kernel(act, grad, out, sems):
        jobs = [
            pltpu.make_async_copy(act, out.at[:, :depth], sems.at[0]),
            pltpu.make_async_copy(grad, out.at[:, depth:], sems.at[1]),
        ]
        for job in jobs:
            job.start()
        for job in jobs:
            job.wait()

    return pl.pallas_call(
        kernel,
        in_specs=[pl.BlockSpec(memory_space=pl.ANY)] * 2,
        out_specs=pl.BlockSpec(memory_space=pl.ANY),
        out_shape=jax.ShapeDtypeStruct((act.shape[0], depth + width), act.dtype),
        scratch_shapes=[pltpu.SemaphoreType.DMA((2,))],
        compiler_params=params(PACK_LIMIT),
        name="pack",
    )(act, grad)


def call(kernel, outs, *operands, **more):
    shapes = tuple(jax.ShapeDtypeStruct(out, jnp.bfloat16) for out in outs)
    name = kernel.__name__
    return pl.pallas_call(kernel, out_shape=shapes, compiler_params=params(), name=name, **more)(*operands)


def body(act, grad, weight):
    depth = act.shape[1]
    width = grad.shape[1]
    deep = weight.shape[0]
    packed = pack(act, grad)
    packed_other = shift(packed, "c", 1, C)
    rows = depth // X
    before = pl.pallas_call(
        functools.partial(own_product, depth),
        out_shape=jax.ShapeDtypeStruct((X, 2, rows, 128), jnp.float32),
        compiler_params=params(),
        name="own_product",
    )(packed)
    partial = pl.pallas_call(
        functools.partial(pair_product, depth),
        out_specs=pl.BlockSpec(memory_space=pl.ANY),
        out_shape=jax.ShapeDtypeStruct((X * rows, 256), jnp.bfloat16),
        scratch_shapes=[
            pltpu.VMEM((X, 2, rows, 128), jnp.float32),
            pltpu.VMEM((X, rows, 256), jnp.bfloat16),
            pltpu.SemaphoreType.DMA((X,)),
        ],
        compiler_params=params(),
        name="pair_product",
    )(packed_other, before)
    partial = partial.reshape(X * Y, rows // Y, 256)
    parts = all_to_all(partial, ("x", "y"), PLANE)

    def towards(axes, size, step):
        return axes + ("c",), [(((i + step - 2 * step * c) % size) * C + c, i * C + c) for i in range(size) for c in range(C)]

    def swap(a):
        return shift(a, "c", 1, C)

    unit = (deep, width)
    (held,) = call(
        hold,
        [unit],
        weight,
        partial,
        in_specs=[pl.BlockSpec(memory_space=pltpu.VMEM), pl.BlockSpec(memory_space=pl.ANY)],
        cost_estimate=BUSY,
    )
    column = lax.all_gather(held, ("zl", "c"), axis=0, tiled=True).reshape((ZL, C) + unit)
    (half,) = call(own_half, [(ZL,) + unit], column)
    near = lax.ppermute(column, *towards(("y",), Y, 1))
    far = lax.ppermute(half, *towards(("y",), Y, 2))

    chip_sum = pl.pallas_call(
        sum_chips,
        out_shape=jax.ShapeDtypeStruct((Z * C, 8, 256), jnp.bfloat16),
        scratch_shapes=[pltpu.VMEM((2, 208, 128), jnp.float32)],
        compiler_params=params(),
        name="sum_chips",
    )(parts)
    planes = all_to_all(chip_sum, ("zh", "zl", "c"), COLUMN)

    low, high = call(in_two, [(2, C) + unit] * 2, near)
    input_grad, done = pl.pallas_call(
        input_product,
        out_shape=(jax.ShapeDtypeStruct(act.shape, jnp.bfloat16), jax.ShapeDtypeStruct((8, 128), jnp.float32)),
        compiler_params=params(),
        name="input_product",
    )(grad, column, near, far, swap(low), swap(high), swap(far))
    weight_grad = pl.pallas_call(
        sum_planes,
        in_specs=[pl.BlockSpec(memory_space=pltpu.VMEM), pl.BlockSpec(memory_space=pl.ANY)],
        out_shape=jax.ShapeDtypeStruct((5, 512), jnp.float32),
        compiler_params=params(),
        name="sum_planes",
    )(planes, done)
    return input_grad, weight_grad


def solution(mesh):
    fine = Mesh(mesh.devices.reshape(X, ZH, ZL, Y, C), ("x", "zh", "zl", "y", "c"))
    every = P(("x", "zh", "zl", "y", "c"), None)
    return jax.shard_map(
        body,
        mesh=fine,
        in_specs=(every, every, P(("zl", "y", "c"), None)),
        out_specs=(every, every),
        check_vma=False,
    )
```

```python
import functools

import jax
import jax.numpy as jnp
from jax import lax
from jax.experimental import pallas as pl
from jax.experimental.pallas import tpu as pltpu
from jax.sharding import Mesh, PartitionSpec as P

X, ZH, ZL, Y, C = 4, 4, 4, 4, 2
Z = ZH * ZL
VMEM_LIMIT = 48 * 1024 * 1024
PACK_LIMIT = 62_200_000

BUSY = pl.CostEstimate(flops=20_000_000_000, bytes_accessed=50_000_000, transcendentals=0)

FIRST_Z = 10
PLANE = list(range(X * Y))[::-1]
COLUMN = [((FIRST_Z + i) % Z) * C + c for i in range(Z) for c in range(C)]

NT = (((1,), (1,)), ((), ()))
TN = (((0,), (0,)), ((), ()))


def dot(a, b, dims):
    return lax.dot_general(a, b, dims, preferred_element_type=jnp.float32)


def all_to_all(a, axes, order):
    return lax.all_to_all(a, axes, split_axis=0, concat_axis=0, tiled=True, axis_index_groups=[order])


def shift(a, axes, step, size):
    return lax.ppermute(a, axes, [(i, (i + step) % size) for i in range(size)])


def own_product(depth, own, total):
    half = pl.ds(pl.multiple_of(depth + lax.axis_index("c") * 256, 128), 256)
    rows = depth // X
    for x in range(X):
        product = dot(own[:, x * rows : (x + 1) * rows], own[:, half], TN)
        for lane in range(2):
            total[x, lane] = product[:, lane * 128 : (lane + 1) * 128]


def pair_product(depth, other, before, out, total, ready, sems):
    half = pl.ds(pl.multiple_of(depth + lax.axis_index("c") * 256, 128), 256)
    rows = depth // X
    jobs = []
    for x in range(X):
        blocks = [PLANE.index(x * Y + y) for y in range(Y)]
        product = dot(other[:, x * rows : (x + 1) * rows], other[:, half], TN)
        for lane in range(2):
            lanes = slice(lane * 128, (lane + 1) * 128)
            total[x, lane] = product[:, lanes] + before[x, lane]
            for row in range(10 * Y):
                place = (blocks[row // 10] - min(blocks)) * 10 + row % 10
                taken = total[x, lane, pl.ds(row, Z, stride=10 * Y), :]
                ready[x, place * Z : (place + 1) * Z, lanes] = taken.astype(jnp.bfloat16)
        target = out.at[pl.ds(min(blocks) * 10 * Z, rows)]
        jobs.append(pltpu.make_async_copy(ready.at[x], target, sems.at[x]))
        jobs[-1].start()
    for job in jobs:
        job.wait()


def sum_chips(parts, out, total):
    rows = parts.shape[1]
    summed = jnp.sum(parts[...].astype(jnp.float32), axis=0)
    for lane in range(2):
        lanes = slice(lane * 128, (lane + 1) * 128)
        total[lane, :rows] = summed[:, lanes]
        total[lane, rows:] = jnp.zeros((total.shape[1] - rows, 128), jnp.float32)
        for z in range(Z):
            for core in range(C):
                out[COLUMN.index(z * C + core), :, lanes] = total[lane, pl.ds(core * 5 * Z + z, 8, stride=Z), :].astype(jnp.bfloat16)


def sum_planes(parts, after, out):
    total = jnp.sum(parts[...].astype(jnp.float32).reshape(Z, C, 8, 256), axis=0)
    out[:, :256] = total[0, :5]
    out[:, 256:] = total[1, :5]


def hold(weight, after, out):
    out[...] = weight[...]


def own_half(column, out):
    core = lax.axis_index("c")
    for step in range(ZL):
        out[step] = jnp.where(core == 0, column[step, 0], column[step, 1])


def in_two(near, low, high):
    low[...] = near[:2]
    high[...] = near[2:]


def input_product(grad, column, near, far, low, high, far_other, out, done):
    me, core = lax.axis_index("y"), lax.axis_index("c")
    first = core == 0
    for step in range(ZL):
        near_other = (low, high)[step // 2][step % 2]
        far_two = jnp.where(first, far[step], far_other[step]), jnp.where(first, far_other[step], far[step])
        ahead = [
            column[step],
            jnp.where(first, near[step], near_other),
            jnp.stack(far_two),
            jnp.where(first, near_other, near[step]),
        ]
        for bit in (1, 2):
            turned = ahead[-bit:] + ahead[:-bit]
            ahead = [jnp.where((me & bit) != 0, a, b) for a, b in zip(turned, ahead)]
        block = jnp.concatenate([rows[c] for rows in ahead for c in range(C)], axis=0)
        out[:, step * 640 : (step + 1) * 640] = dot(grad[...], block, NT).astype(jnp.bfloat16)
    done[...] = jnp.zeros(done.shape, done.dtype)


def params(limit=VMEM_LIMIT):
    return pltpu.CompilerParams(vmem_limit_bytes=limit)


def pack(act, grad):
    depth, width = act.shape[1], grad.shape[1]

    def kernel(act, grad, out, sems):
        jobs = [
            pltpu.make_async_copy(act, out.at[:, :depth], sems.at[0]),
            pltpu.make_async_copy(grad, out.at[:, depth:], sems.at[1]),
        ]
        for job in jobs:
            job.start()
        for job in jobs:
            job.wait()

    return pl.pallas_call(
        kernel,
        in_specs=[pl.BlockSpec(memory_space=pl.ANY)] * 2,
        out_specs=pl.BlockSpec(memory_space=pltpu.VMEM),
        out_shape=jax.ShapeDtypeStruct((act.shape[0], depth + width), act.dtype),
        scratch_shapes=[pltpu.SemaphoreType.DMA((2,))],
        compiler_params=params(PACK_LIMIT),
        name="pack",
    )(act, grad)


def call(kernel, outs, *operands, **more):
    shapes = tuple(jax.ShapeDtypeStruct(out, jnp.bfloat16) for out in outs)
    name = kernel.__name__
    return pl.pallas_call(kernel, out_shape=shapes, compiler_params=params(), name=name, **more)(*operands)


def body(act, grad, weight):
    depth = act.shape[1]
    width = grad.shape[1]
    deep = weight.shape[0]
    packed = pack(act, grad)
    packed_other = shift(packed, "c", 1, C)
    rows = depth // X
    before = pl.pallas_call(
        functools.partial(own_product, depth),
        out_shape=jax.ShapeDtypeStruct((X, 2, rows, 128), jnp.float32),
        compiler_params=params(),
        name="own_product",
    )(packed)
    partial = pl.pallas_call(
        functools.partial(pair_product, depth),
        out_specs=pl.BlockSpec(memory_space=pl.ANY),
        out_shape=jax.ShapeDtypeStruct((X * rows, 256), jnp.bfloat16),
        scratch_shapes=[
            pltpu.VMEM((X, 2, rows, 128), jnp.float32),
            pltpu.VMEM((X, rows, 256), jnp.bfloat16),
            pltpu.SemaphoreType.DMA((X,)),
        ],
        compiler_params=params(),
        name="pair_product",
    )(packed_other, before)
    partial = partial.reshape(X * Y, rows // Y, 256)
    parts = all_to_all(partial, ("x", "y"), PLANE)

    def towards(axes, size, step):
        return axes + ("c",), [(((i + step - 2 * step * c) % size) * C + c, i * C + c) for i in range(size) for c in range(C)]

    def swap(a):
        return shift(a, "c", 1, C)

    unit = (deep, width)
    (held,) = call(
        hold,
        [unit],
        weight,
        partial,
        in_specs=[pl.BlockSpec(memory_space=pltpu.VMEM), pl.BlockSpec(memory_space=pl.ANY)],
        cost_estimate=BUSY,
    )
    column = lax.all_gather(held, ("zl", "c"), axis=0, tiled=True).reshape((ZL, C) + unit)
    (half,) = call(own_half, [(ZL,) + unit], column)
    near = lax.ppermute(column, *towards(("y",), Y, 1))
    far = lax.ppermute(half, *towards(("y",), Y, 2))

    chip_sum = pl.pallas_call(
        sum_chips,
        out_shape=jax.ShapeDtypeStruct((Z * C, 8, 256), jnp.bfloat16),
        scratch_shapes=[pltpu.VMEM((2, 208, 128), jnp.float32)],
        compiler_params=params(),
        name="sum_chips",
    )(parts)
    planes = all_to_all(chip_sum, ("zh", "zl", "c"), COLUMN)

    low, high = call(in_two, [(2, C) + unit] * 2, near)
    input_grad, done = pl.pallas_call(
        input_product,
        out_shape=(jax.ShapeDtypeStruct(act.shape, jnp.bfloat16), jax.ShapeDtypeStruct((8, 128), jnp.float32)),
        compiler_params=params(),
        name="input_product",
    )(grad, column, near, far, swap(low), swap(high), swap(far))
    weight_grad = pl.pallas_call(
        sum_planes,
        in_specs=[pl.BlockSpec(memory_space=pltpu.VMEM), pl.BlockSpec(memory_space=pl.ANY)],
        out_shape=jax.ShapeDtypeStruct((5, 512), jnp.float32),
        compiler_params=params(),
        name="sum_planes",
    )(planes, done)
    return input_grad, weight_grad


def solution(mesh):
    fine = Mesh(mesh.devices.reshape(X, ZH, ZL, Y, C), ("x", "zh", "zl", "y", "c"))
    every = P(("x", "zh", "zl", "y", "c"), None)
    return jax.shard_map(
        body,
        mesh=fine,
        in_specs=(every, every, P(("zl", "y", "c"), None)),
        out_specs=(every, every),
        check_vma=False,
    )
```
